32 devices in a mesh: dp: 4 (over x, core), tensor: 8 (over z, y).
Axes of the slice: x: 2, y: 2, z: 4, core: 2. Of those that a mesh axis runs over, the one named last changes fastest.
Arguments:
- old_m_codes: bfloat16 [4096, 2048], P(('dp', 'tensor')), may hold values from -1 to 1
- old_m_scale: float32 [4096], P(('dp', 'tensor')), may hold values from 0.3 to 3
- old_v_codes: bfloat16 [4096, 2048], P(('dp', 'tensor')), may hold values from 0.019897461 to 1
- old_v_scale: float32 [4096], P(('dp', 'tensor')), may hold values from 1 to 10
- block_target: int32 [4096], replicated, may hold values from 0 to 4095, as said below
- new_offset: int32 [32], P(('dp', 'tensor')), may hold values from 128 to 1920, as said below
- grad_part: bfloat16 [4, 8, 512, 2048], P('dp', 'tensor'), may hold values from -6 to 6
- master_weight: float32 [8, 512, 2048], P('tensor', 'dp'), may hold values from -6 to 6
Outputs:
- new_m_codes: bfloat16 [8, 512, 2048], P('tensor', 'dp')
- new_m_scale: float32 [32, 129], P(('dp', 'tensor'))
- new_v_codes: bfloat16 [8, 512, 2048], P('tensor', 'dp')
- new_v_scale: float32 [32, 129], P(('dp', 'tensor'))
- adam_update: float32 [8, 512, 2048], P('tensor', 'dp')
- new_weight: bfloat16 [8, 512, 2048], P('tensor', 'dp')
The draws below stay inside these ranges and needn't reach their ends.
Inputs may be any that keep to these rules, and one draw needn't show every extreme that they name: block_target is a bijection of the old blocks onto the new ones. Device n along dp+tensor holds old blocks n * 128 to (n+1) * 128 - 1. At most 8 old blocks of one device go to one new owner, and exactly 8 for some pairs. `new_offset`: multiples of 128.
All inputs are finite; a program needn't handle non-finite values. Where the reference program divides by a largest or mean magnitude, that divisor is 1e-20 or more.
Results may differ from the reference program's by a relative error of at most 0.013.
Values may be sent and summed in bfloat16 or wider, within the bound.
A program may use at most 128 MiB of HBM per device.

```python
import math
import jax
import jax.numpy as jnp
from jax import lax

BLOCK_SIZE = 2048
HELD_BLOCKS = 128
OWNERS = 32
ALL_BLOCKS = 4096
CAPACITY = 8
N_DP = 4
N_TENSOR = 8


def permute_slots(key):
    return jax.random.permutation(key, HELD_BLOCKS)


def draw_block_target(key, part):
    key = jax.random.fold_in(key, 11)
    first, second, third, fourth = jax.random.split(key, 4)
    sigma = jax.random.permutation(first, OWNERS)
    shifts = jax.random.permutation(second, OWNERS)
    rotation = jax.random.randint(third, (OWNERS,), 0, HELD_BLOCKS)
    slot_order = jax.vmap(permute_slots)(jax.random.split(fourth, OWNERS))
    full_count = max(1, HELD_BLOCKS // (2 * CAPACITY))
    remaining = OWNERS - full_count
    local = jnp.arange(HELD_BLOCKS)
    rotated = (local[None, :] + rotation[:, None]) % HELD_BLOCKS
    classes = jnp.where(rotated < full_count * CAPACITY, rotated // CAPACITY, full_count + (rotated - full_count * CAPACITY) % remaining)
    owner = (sigma[:, None] + shifts[classes]) % OWNERS
    slots = slot_order[owner, rotated]
    return (owner * HELD_BLOCKS + slots).reshape(-1).astype(jnp.int32)


def draw_new_offset(key, part):
    key = jax.random.fold_in(key, 23)
    order = jax.random.permutation(key, OWNERS)
    return (BLOCK_SIZE // 16 * (1 + order % 15)).astype(jnp.int32)


def strengthened(drawn, stream_key, source, target, parts, factor):
    owner, partner = [(jnp.arange(drawn.shape[axis_at]) // (drawn.shape[axis_at] // parts)).reshape([-1 if axis == axis_at else 1 for axis in range(drawn.ndim)]) for axis_at in (source, target)]
    chosen = jax.random.permutation(stream_key, parts)[partner]
    strong = (owner == chosen) | (owner == (partner + parts // 2) % parts)
    return jnp.where(strong, factor * drawn, drawn)


def level_of(own_key, dims, shards, least, largest):
    loudness, own = 1.0, jax.random.fold_in(own_key, 6)
    for dim, shards_of in shards:
        draws = jnp.exp(jax.random.uniform(jax.random.fold_in(own, dim), (shards_of,), jnp.float32, least / len(shards), largest / len(shards)))
        loudness = loudness * jnp.repeat(draws, dims[dim] // shards_of).reshape([-1 if axis == dim else 1 for axis in range(len(dims))])
    return loudness


def gaussian(rng, shape, scale, bound, shards=(), kind=jnp.bfloat16):
    entries = scale * jax.random.normal(rng, shape, jnp.float32)
    if shards:
        entries = entries * level_of(rng, shape, shards, -0.22, 0.18)
    return jnp.clip(entries, -bound, bound).astype(kind)


def heavy_noise(stream_key, extent, scale, reach, pieces, heavy, dtype=jnp.bfloat16):
    array = scale * jax.random.normal(stream_key, extent, jnp.float32)
    if pieces:
        array = array * level_of(stream_key, extent, pieces, -0.22, 0.18)
    return jnp.clip(strengthened(array, jax.random.fold_in(stream_key, 3), *heavy), -reach, reach).astype(dtype)


def setup_inputs(seed: int = 0) -> dict:
    seeds = jax.random.split(jax.random.key(seed), 9)
    return {
        "old_m_codes": jnp.clip(jax.random.uniform(seeds[0], (ALL_BLOCKS, BLOCK_SIZE), jnp.float32, -1.0, 1.0) * level_of(seeds[0], (ALL_BLOCKS, BLOCK_SIZE), ((0, 32),), -0.4, 0.0), -1.0, 1.0).astype(jnp.bfloat16),
        "old_m_scale": jnp.clip(jnp.exp(math.log(3.0) - 2.3025851 * jax.random.uniform(seeds[1], (ALL_BLOCKS,), jnp.float32) ** level_of(seeds[1], (ALL_BLOCKS,), ((0, 32),), -0.2, 0.2)), 0.3, 3.0),
        "old_v_codes": jnp.clip(0.019897461 + 0.98010254 * jax.random.uniform(seeds[2], (ALL_BLOCKS, BLOCK_SIZE), jnp.float32) ** level_of(seeds[2], (ALL_BLOCKS, BLOCK_SIZE), ((0, 32),), -0.2, 0.2), 0.019897461, 1.0).astype(jnp.bfloat16),
        "old_v_scale": jnp.clip(jnp.exp(math.log(10.0) - 2.3025851 * jax.random.uniform(seeds[3], (ALL_BLOCKS,), jnp.float32) ** level_of(seeds[3], (ALL_BLOCKS,), ((0, 32),), -0.2, 0.2)), 1.0, 10.0),
        "block_target": draw_block_target(jax.random.fold_in(seeds[8], 71), 0),
        "new_offset": draw_new_offset(jax.random.fold_in(seeds[8], 71), 0),
        "grad_part": heavy_noise(seeds[6], (N_DP, N_TENSOR, N_DP * HELD_BLOCKS, BLOCK_SIZE), 1.0, 6.0, ((0, 4), (1, 8)), (0, 2, 4, 2.0)),
        "master_weight": gaussian(seeds[7], (N_TENSOR, N_DP * HELD_BLOCKS, BLOCK_SIZE), 1.0, 6.0, ((0, 8), (1, 4)), jnp.float32),
    }


FIRST_DECAY = 0.9
SECOND_DECAY = 0.95
FIRST_CORRECTION = 1.0 - 0.9 ** 40
SECOND_CORRECTION = 1.0 - 0.95 ** 40
ADAM_EPSILON = 1e-08
WEIGHT_DECAY = 0.1
LEARN_RATE = 6e-05

def requantize(flat, offset, held, size):
    start = size - offset
    padded = lax.dynamic_update_slice(jnp.zeros(((held + 1) * size,), jnp.float32), flat, (start,))
    blocks = padded.reshape(held + 1, size)
    scales = lax.optimization_barrier(jnp.max(jnp.abs(blocks), axis=1)) + 1e-06
    codes = (blocks / scales[:, None]).reshape(-1)
    return (lax.dynamic_slice(codes, (start,), (held * size,)).astype(jnp.bfloat16), scales)

def requant_pair(pair):
    return requantize(pair[0], pair[1], HELD_BLOCKS, BLOCK_SIZE)

def relayout(values):
    return values.reshape(N_DP, N_TENSOR, HELD_BLOCKS, BLOCK_SIZE).transpose(1, 0, 2, 3).reshape(N_TENSOR, N_DP * HELD_BLOCKS, BLOCK_SIZE)

def owner_major(values):
    return values.reshape(N_TENSOR, N_DP, HELD_BLOCKS * BLOCK_SIZE).transpose(1, 0, 2).reshape(N_DP * N_TENSOR, HELD_BLOCKS * BLOCK_SIZE)

def reference(old_m_codes, old_m_scale, old_v_codes, old_v_scale, block_target, new_offset, grad_part, master_weight):
    m_old = old_m_codes.astype(jnp.float32) * old_m_scale[:, None]
    v_old = old_v_codes.astype(jnp.float32) * old_v_scale[:, None]
    m_prev = relayout(jnp.zeros_like(m_old).at[block_target].set(m_old))
    v_prev = relayout(jnp.zeros_like(v_old).at[block_target].set(v_old))
    grad = grad_part[0].astype(jnp.float32)
    for replica in range(1, N_DP):
        grad = grad + grad_part[replica].astype(jnp.float32)
    m_next = FIRST_DECAY * m_prev + (1.0 - FIRST_DECAY) * grad
    v_next = SECOND_DECAY * v_prev + (1.0 - SECOND_DECAY) * grad * grad
    adam_update = m_next / FIRST_CORRECTION / (jnp.sqrt(v_next / SECOND_CORRECTION) + ADAM_EPSILON) + WEIGHT_DECAY * master_weight
    new_weight = (master_weight - LEARN_RATE * adam_update).astype(jnp.bfloat16)
    m_codes, m_scale = lax.map(requant_pair, (owner_major(m_next), new_offset))
    v_codes, v_scale = lax.map(requant_pair, (owner_major(v_next), new_offset))
    return (relayout(m_codes), m_scale, relayout(v_codes), v_scale, adam_update, new_weight)
```

```python
import functools

import jax
import jax.numpy as jnp
from jax import lax
from jax.experimental import pallas as pl
from jax.experimental.pallas import tpu as pltpu
from jax.sharding import PartitionSpec as P

FIRST_DECAY = 0.9
SECOND_DECAY = 0.95
FIRST_CORRECTION = 1.0 - 0.9**40
SECOND_CORRECTION = 1.0 - 0.95**40
ADAM_EPSILON = 1e-08
WEIGHT_DECAY = 0.1
LEARN_RATE = 6e-05
MESH = pl.DeviceIdType.MESH


def column_of(row, held):
    return jnp.broadcast_to(row, (held, held)).T


def exchange(
    n_dp,
    n_tensor,
    capacity,
    targets_ref,
    m_codes_ref,
    m_scale_ref,
    v_codes_ref,
    v_scale_ref,
    grad_ref,
    arrived_ref,
    grads_ref,
    route_ref,
    outgoing,
    send_sem,
    recv_sem,
    grad_send_sem,
    grad_recv_sem,
    local_sem,
):
    owners = n_dp * n_tensor
    held, size = m_codes_ref.shape
    rows = outgoing.shape[1]
    my_dp = lax.axis_index("dp")
    my_tensor = lax.axis_index("tensor")
    myself = my_dp * n_tensor + my_tensor

    barrier = pltpu.get_barrier_semaphore()

    def greet(step, carry):
        other = lax.rem(myself + step, owners)
        pl.semaphore_signal(
            barrier, inc=1, device_id=(other // n_tensor, lax.rem(other, n_tensor)), device_id_type=MESH
        )
        return carry

    lax.fori_loop(1, owners, greet, 0)

    mine = targets_ref[pl.ds(myself, 1), :]
    owner = (mine // held).astype(jnp.float32)
    owner_col = column_of(owner, held)
    owner_row = jnp.broadcast_to(owner, (held, held))
    down = lax.broadcasted_iota(jnp.int32, (held, held), 0)
    across = lax.broadcasted_iota(jnp.int32, (held, held), 1)
    rank = jnp.sum(
        jnp.where((owner_col == owner_row) & (down < across), 1.0, 0.0), axis=0, keepdims=True
    )
    slot = (owner * rows + rank).astype(jnp.int32)
    slots = jnp.concatenate([slot, slot + capacity], axis=1)
    m_old = m_codes_ref[...].astype(jnp.float32) * column_of(m_scale_ref[...], held)[:, :1]
    v_old = v_codes_ref[...].astype(jnp.float32) * column_of(v_scale_ref[...], held)[:, :1]
    moments = jnp.concatenate([m_old.astype(jnp.bfloat16), v_old.astype(jnp.bfloat16)], axis=0)
    some = 8
    for first in range(0, owners, some):
        place = lax.broadcasted_iota(jnp.int32, (some * rows, 2 * held), 0) + first * rows
        chosen = jnp.where(place == slots, 1.0, 0.0).astype(jnp.bfloat16)
        packed = jnp.dot(chosen, moments, preferred_element_type=jnp.float32)
        outgoing[first : first + some] = packed.astype(jnp.bfloat16).reshape(some, rows, size)

    pl.semaphore_wait(barrier, owners - 1)

    def grad_copy(step):
        other = lax.rem(my_dp + step, n_dp)
        return pltpu.make_async_remote_copy(
            src_ref=grad_ref.at[pl.ds(pl.multiple_of(other * held, held), held)],
            dst_ref=grads_ref.at[my_dp],
            send_sem=grad_send_sem.at[other],
            recv_sem=grad_recv_sem.at[my_dp],
            device_id=(other, my_tensor),
            device_id_type=MESH,
        )

    def grad_arrival(step):
        other = lax.rem(my_dp + step, n_dp)
        return pltpu.make_async_remote_copy(
            src_ref=grad_ref.at[pl.ds(pl.multiple_of(other * held, held), held)],
            dst_ref=grads_ref.at[other],
            send_sem=grad_send_sem.at[other],
            recv_sem=grad_recv_sem.at[other],
            device_id=(other, my_tensor),
            device_id_type=MESH,
        )

    def peer(step):
        tensor_step = lax.rem(step // n_dp + n_tensor // 2, n_tensor)
        dp_step = lax.rem(step, n_dp)
        there = lax.rem(my_dp + dp_step, n_dp)
        across = lax.rem(my_tensor + tensor_step, n_tensor)
        return there, across, there * n_tensor + across, (tensor_step + dp_step) > 0

    def send(step, carry):
        there, across, other, remote = peer(step)

        @pl.when(remote)
        def _():
            pltpu.make_async_remote_copy(
                src_ref=outgoing.at[other],
                dst_ref=arrived_ref.at[myself],
                send_sem=send_sem.at[other],
                recv_sem=recv_sem.at[myself],
                device_id=(there, across),
                device_id_type=MESH,
            ).start()

        return carry

    def finish(step, carry):
        there, across, other, remote = peer(step)

        @pl.when(remote)
        def _():
            copy = pltpu.make_async_remote_copy(
                src_ref=outgoing.at[other],
                dst_ref=arrived_ref.at[other],
                send_sem=send_sem.at[other],
                recv_sem=recv_sem.at[other],
                device_id=(there, across),
                device_id_type=MESH,
            )
            copy.wait_send()
            copy.wait_recv()

        return carry

    lax.fori_loop(0, owners, send, 0)
    for step in range(1, n_dp):
        grad_copy(step).start()
    own_grad = pltpu.make_async_copy(
        grad_ref.at[pl.ds(pl.multiple_of(my_dp * held, held), held)], grads_ref.at[my_dp], local_sem.at[0]
    )
    own_grad.start()
    own_slots = pltpu.make_async_copy(outgoing.at[myself], arrived_ref.at[myself], local_sem.at[1])
    own_slots.start()

    targets = targets_ref[...]
    is_mine = jnp.where(targets // held == myself, 1.0, 0.0)
    before = jnp.where(down < across, 1.0, 0.0).astype(jnp.bfloat16)
    ranks = jnp.dot(is_mine.astype(jnp.bfloat16), before, preferred_element_type=jnp.float32)
    ranks = jnp.where(is_mine > 0.0, ranks, -1.0)
    row = lax.rem(targets, held).astype(jnp.float32) + 1.0

    def spread(x):
        return jnp.broadcast_to(x[:, None, :], (owners, rows, held)).reshape(owners * rows, held)

    index = lax.broadcasted_iota(jnp.int32, (owners, rows, held), 1).reshape(owners * rows, held)
    within = jnp.where(index >= capacity, index - capacity, index)
    hit = jnp.where(spread(ranks) == within.astype(jnp.float32), spread(row), 0.0)
    place = jnp.sum(hit, axis=1, keepdims=True).astype(jnp.int32) - 1
    index = index[:, :1]
    place = jnp.where((place >= 0) & (index >= capacity), place + held, place)
    place = jnp.where(index < 2 * capacity, place, -1)
    wanted = lax.broadcasted_iota(jnp.int32, (owners * rows, 2 * held), 1)
    route_ref[...] = jnp.where(place == wanted, 1.0, 0.0).T.astype(jnp.bfloat16)

    for step in range(1, n_dp):
        grad_copy(step).wait_send()
        grad_arrival(step).wait_recv()
    own_grad.wait()
    own_slots.wait()
    lax.fori_loop(0, owners, finish, 0)


def update(
    n_dp,
    offset_ref,
    route_ref,
    arrived_ref,
    grads_ref,
    master_ref,
    m_codes_ref,
    m_scale_ref,
    v_codes_ref,
    v_scale_ref,
    adam_ref,
    weight_ref,
    m_all,
    v_all,
    peaks,
):
    step = pl.program_id(0)
    held, width = master_ref.shape
    offset = offset_ref[0]
    placed = jnp.dot(route_ref[...], arrived_ref[...], preferred_element_type=jnp.float32)
    grad = grads_ref[0].astype(jnp.float32)
    for replica in range(1, n_dp):
        grad = grad + grads_ref[replica].astype(jnp.float32)
    m_next = FIRST_DECAY * placed[:held] + (1.0 - FIRST_DECAY) * grad
    v_next = SECOND_DECAY * placed[held:] + (1.0 - SECOND_DECAY) * grad * grad
    master = master_ref[...]
    adam = (m_next * (1.0 / FIRST_CORRECTION)) / (
        jnp.sqrt(v_next * (1.0 / SECOND_CORRECTION)) + ADAM_EPSILON
    ) + WEIGHT_DECAY * master
    adam_ref[...] = adam
    weight_ref[...] = (master - LEARN_RATE * adam).astype(jnp.bfloat16)
    m_all[step] = m_next
    v_all[step] = v_next
    column = lax.broadcasted_iota(jnp.int32, (held, width), 1)
    head = column < offset - step * width

    @pl.when(step == 0)
    def _():
        peaks[...] = jnp.zeros_like(peaks)

    for at, values in ((0, m_next), (2, v_next)):
        size = jnp.abs(values)
        fore = jnp.where(head, size, 0.0)
        rear = jnp.where(head, 0.0, size)
        for part, half in ((0, fore), (1, rear)):
            best = peaks[at + part]
            for lane in range(0, width, 128):
                best = jnp.maximum(best, half[:, lane : lane + 128])
            peaks[at + part] = best

    @pl.when(step == pl.num_programs(0) - 1)
    def _():
        line = lax.broadcasted_iota(jnp.int32, (held, held), 0)
        for at, values, codes_ref, scale_ref in (
            (0, m_all, m_codes_ref, m_scale_ref),
            (2, v_all, v_codes_ref, v_scale_ref),
        ):
            fore = jnp.broadcast_to(jnp.max(peaks[at], axis=1, keepdims=True), (held, held))
            rear = jnp.broadcast_to(jnp.max(peaks[at + 1], axis=1, keepdims=True), (held, held))
            above = jnp.where(line == 0, 0.0, pltpu.roll(rear, 1, 0))
            below = jnp.where(line == held - 1, 0.0, pltpu.roll(fore, held - 1, 0))
            first = jnp.maximum(above, fore) + 1e-06
            second = jnp.maximum(rear, below) + 1e-06
            scale_ref[:, :held] = first.T[:1, :]
            scale_ref[:, held : held + 1] = second[held - 1 :, :1]
            first = (1.0 / first)[:, :1]
            second = (1.0 / second)[:, :1]
            for part in range(values.shape[0]):
                left = column < offset - part * width
                codes_ref[:, part * width : (part + 1) * width] = (
                    values[part] * jnp.where(left, first, second)
                ).astype(jnp.bfloat16)


def local(
    n_dp,
    n_tensor,
    old_m_codes,
    old_m_scale,
    old_v_codes,
    old_v_scale,
    block_target,
    new_offset,
    grad_part,
    master_weight,
):
    owners = n_dp * n_tensor
    held, size = old_m_codes.shape
    capacity = max(2, 2 * held // owners)
    rows = -(-2 * capacity // 16) * 16
    vmem = pl.BlockSpec(memory_space=pltpu.VMEM)
    hbm = pl.BlockSpec(memory_space=pl.ANY)
    arrived, grads, route = pl.pallas_call(
        functools.partial(exchange, n_dp, n_tensor, capacity),
        out_shape=(
            jax.ShapeDtypeStruct((owners, rows, size), jnp.bfloat16),
            jax.ShapeDtypeStruct((n_dp, held, size), jnp.bfloat16),
            jax.ShapeDtypeStruct((2 * held, owners * rows), jnp.bfloat16),
        ),
        in_specs=[vmem] * 5 + [hbm],
        out_specs=(hbm, hbm, vmem),
        scratch_shapes=[
            pltpu.VMEM((owners, rows, size), jnp.bfloat16),
            pltpu.SemaphoreType.DMA((owners,)),
            pltpu.SemaphoreType.DMA((owners,)),
            pltpu.SemaphoreType.DMA((n_dp,)),
            pltpu.SemaphoreType.DMA((n_dp,)),
            pltpu.SemaphoreType.DMA((2,)),
        ],
        compiler_params=pltpu.CompilerParams(
            collective_id=0, has_side_effects=True, vmem_limit_bytes=48 * 1024 * 1024
        ),
    )(
        block_target.reshape(owners, held),
        old_m_codes,
        old_m_scale.reshape(1, held),
        old_v_codes,
        old_v_scale.reshape(1, held),
        grad_part[0, 0],
    )
    width = 512
    whole = lambda shape: pl.BlockSpec(shape, lambda i: (0, 0))
    part = pl.BlockSpec((held, width), lambda i: (0, i))
    m_codes, m_scale, v_codes, v_scale, adam, weight = pl.pallas_call(
        functools.partial(update, n_dp),
        grid=(size // width,),
        out_shape=(
            jax.ShapeDtypeStruct((held, size), jnp.bfloat16),
            jax.ShapeDtypeStruct((1, held + 1), jnp.float32),
            jax.ShapeDtypeStruct((held, size), jnp.bfloat16),
            jax.ShapeDtypeStruct((1, held + 1), jnp.float32),
            jax.ShapeDtypeStruct((held, size), jnp.float32),
            jax.ShapeDtypeStruct((held, size), jnp.bfloat16),
        ),
        in_specs=[
            pl.BlockSpec(memory_space=pltpu.SMEM),
            whole((2 * held, owners * rows)),
            pl.BlockSpec((owners * rows, width), lambda i: (0, i)),
            pl.BlockSpec((n_dp, held, width), lambda i: (0, 0, i)),
            part,
        ],
        out_specs=(
            whole((held, size)),
            whole((1, held + 1)),
            whole((held, size)),
            whole((1, held + 1)),
            part,
            part,
        ),
        scratch_shapes=[
            pltpu.VMEM((size // width, held, width), jnp.float32),
            pltpu.VMEM((size // width, held, width), jnp.float32),
            pltpu.VMEM((4, held, 128), jnp.float32),
        ],
        compiler_params=pltpu.CompilerParams(
            dimension_semantics=("arbitrary",), vmem_limit_bytes=48 * 1024 * 1024
        ),
    )(
        new_offset,
        route,
        arrived.reshape(owners * rows, size),
        grads,
        master_weight[0],
    )
    return (
        m_codes.reshape(1, held, size),
        m_scale,
        v_codes.reshape(1, held, size),
        v_scale,
        adam.reshape(1, held, size),
        weight.reshape(1, held, size),
    )


def solution(mesh):
    return jax.shard_map(
        functools.partial(local, mesh.shape["dp"], mesh.shape["tensor"]),
        mesh=mesh,
        in_specs=(
            P(("dp", "tensor"), None),
            P(("dp", "tensor")),
            P(("dp", "tensor"), None),
            P(("dp", "tensor")),
            P(),
            P(("dp", "tensor")),
            P("dp", "tensor", None, None),
            P("tensor", "dp", None),
        ),
        out_specs=(
            P("tensor", "dp", None),
            P(("dp", "tensor"), None),
            P("tensor", "dp", None),
            P(("dp", "tensor"), None),
            P("tensor", "dp", None),
            P("tensor", "dp", None),
        ),
        check_vma=False,
    )
```

```python
import functools

import jax
import jax.numpy as jnp
from jax import lax
from jax.experimental import pallas as pl
from jax.experimental.pallas import tpu as pltpu
from jax.sharding import PartitionSpec as P

FIRST_DECAY = 0.9
SECOND_DECAY = 0.95
FIRST_CORRECTION = 1.0 - 0.9**40
SECOND_CORRECTION = 1.0 - 0.95**40
ADAM_EPSILON = 1e-08
WEIGHT_DECAY = 0.1
LEARN_RATE = 6e-05
MESH = pl.DeviceIdType.MESH


def column_of(row, held):
    return jnp.broadcast_to(row, (held, held)).T


def exchange(
    n_dp,
    n_tensor,
    capacity,
    targets_hbm,
    m_codes_hbm,
    m_scale_hbm,
    v_codes_hbm,
    v_scale_hbm,
    grad_ref,
    arrived_ref,
    total_ref,
    route_ref,
    targets_ref,
    m_codes_ref,
    m_scale_ref,
    v_codes_ref,
    v_scale_ref,
    outgoing,
    grad_own,
    grad_pair,
    grad_out,
    grad_in,
    total,
    route,
    send_sem,
    recv_sem,
    pair_send_sem,
    pair_recv_sem,
    grad_send_sem,
    grad_recv_sem,
    own_sem,
    local_sem,
):
    owners = n_dp * n_tensor
    held, size = m_codes_ref.shape
    rows = outgoing.shape[1]
    n_x = n_dp // 2
    my_dp = lax.axis_index("dp")
    my_tensor = lax.axis_index("tensor")
    myself = my_dp * n_tensor + my_tensor
    my_x = my_dp // 2
    my_core = lax.rem(my_dp, 2)

    barrier = pltpu.get_barrier_semaphore()

    def greet(step, carry):
        other = lax.rem(myself + step, owners)
        pl.semaphore_signal(
            barrier, inc=1, device_id=(other // n_tensor, lax.rem(other, n_tensor)), device_id_type=MESH
        )
        return carry

    loads = [
        pltpu.make_async_copy(source, target, local_sem.at[i])
        for i, (source, target) in enumerate(
            (
                (targets_hbm, targets_ref),
                (m_scale_hbm, m_scale_ref),
                (v_scale_hbm, v_scale_ref),
                (m_codes_hbm, m_codes_ref),
                (v_codes_hbm, v_codes_ref),
            )
        )
    ]
    for load in loads:
        load.start()
    lax.fori_loop(1, owners, greet, 0)

    def share(x, core):
        return grad_ref.at[pl.ds(pl.multiple_of((2 * x + core) * held, held), held)]

    own_loads = [
        pltpu.make_async_copy(share(x, my_core), grad_own.at[x], own_sem.at[x]) for x in range(n_x)
    ]
    for load in own_loads:
        load.start()

    loads[0].wait()
    mine = targets_ref[pl.ds(myself, 1), :]
    owner = (mine // held).astype(jnp.float32)
    owner_col = column_of(owner, held)
    owner_row = jnp.broadcast_to(owner, (held, held))
    down = lax.broadcasted_iota(jnp.int32, (held, held), 0)
    across = lax.broadcasted_iota(jnp.int32, (held, held), 1)
    rank = jnp.sum(
        jnp.where((owner_col == owner_row) & (down < across), 1.0, 0.0), axis=0, keepdims=True
    )
    slot = (owner * rows + rank).astype(jnp.int32)
    slots = jnp.concatenate([slot, slot + capacity], axis=1)
    for load in loads[1:]:
        load.wait()
    m_old = m_codes_ref[...].astype(jnp.float32) * column_of(m_scale_ref[...], held)[:, :1]
    v_old = v_codes_ref[...].astype(jnp.float32) * column_of(v_scale_ref[...], held)[:, :1]
    moments = jnp.concatenate([m_old.astype(jnp.bfloat16), v_old.astype(jnp.bfloat16)], axis=0)

    pair_copies = [
        pltpu.make_async_remote_copy(
            src_ref=share(x, 1 - my_core),
            dst_ref=grad_pair.at[x],
            send_sem=pair_send_sem.at[x],
            recv_sem=pair_recv_sem.at[x],
            device_id=(2 * my_x + 1 - my_core, my_tensor),
            device_id_type=MESH,
        )
        for x in range(n_x)
    ]

    def grad_copy(step):
        other = lax.rem(my_x + step, n_x)
        return pltpu.make_async_remote_copy(
            src_ref=grad_out.at[other],
            dst_ref=grad_in.at[my_x],
            send_sem=grad_send_sem.at[other],
            recv_sem=grad_recv_sem.at[my_x],
            device_id=(2 * other + my_core, my_tensor),
            device_id_type=MESH,
        )

    def grad_arrival(step):
        other = lax.rem(my_x + step, n_x)
        return pltpu.make_async_remote_copy(
            src_ref=grad_out.at[other],
            dst_ref=grad_in.at[other],
            send_sem=grad_send_sem.at[other],
            recv_sem=grad_recv_sem.at[other],
            device_id=(2 * other + my_core, my_tensor),
            device_id_type=MESH,
        )

    def copy_to(there, lane, other, landing, arrival):
        return pltpu.make_async_remote_copy(
            src_ref=outgoing.at[other],
            dst_ref=arrived_ref.at[landing],
            send_sem=send_sem.at[other],
            recv_sem=recv_sem.at[arrival],
            device_id=(there, lane),
            device_id_type=MESH,
        )

    for group in range(n_dp):
        there = lax.rem(my_dp + group + 1, n_dp)
        base = there * n_tensor
        place = lax.broadcasted_iota(jnp.int32, (n_tensor * rows, 2 * held), 0) + base * rows
        chosen = jnp.where(place == slots, 1.0, 0.0).astype(jnp.bfloat16)
        packed = jnp.dot(chosen, moments, preferred_element_type=jnp.float32)
        outgoing[pl.ds(base, n_tensor)] = packed.astype(jnp.bfloat16).reshape(n_tensor, rows, size)
        if group == 0:
            pl.semaphore_wait(barrier, owners - 1)
            for copy in pair_copies:
                copy.start()
        last = group == n_dp - 1

        def send(step, carry, there=there, base=base):
            lane = lax.rem(my_tensor + step, n_tensor)
            copy_to(there, lane, base + lane, myself, myself).start()
            return carry

        half = n_tensor // 2
        lax.fori_loop(half, n_tensor, send, 0)
        lax.fori_loop(1 if last else 0, half, send, 0)
    own_slots = pltpu.make_async_copy(outgoing.at[myself], arrived_ref.at[myself], local_sem.at[5])
    own_slots.start()

    for load in own_loads:
        load.wait()
    for copy in pair_copies:
        copy.wait_send()
        copy.wait_recv()
    for step in range(1, n_x):
        other = lax.rem(my_x + step, n_x)
        grad_out[other] = (
            grad_own[other].astype(jnp.float32) + grad_pair[other].astype(jnp.float32)
        ).astype(jnp.bfloat16)
        grad_copy(step).start()

    targets = targets_ref[...]
    is_mine = jnp.where(targets // held == myself, 1.0, 0.0)
    before = jnp.where(down < across, 1.0, 0.0).astype(jnp.bfloat16)
    ranks = jnp.dot(is_mine.astype(jnp.bfloat16), before, preferred_element_type=jnp.float32)
    ranks = jnp.where(is_mine > 0.0, ranks, -1.0)
    row = lax.rem(targets, held).astype(jnp.float32) + 1.0

    def spread(x):
        return jnp.broadcast_to(x[:, None, :], (owners, rows, held)).reshape(owners * rows, held)

    index = lax.broadcasted_iota(jnp.int32, (owners, rows, held), 1).reshape(owners * rows, held)
    within = jnp.where(index >= capacity, index - capacity, index)
    hit = jnp.where(spread(ranks) == within.astype(jnp.float32), spread(row), 0.0)
    place = jnp.sum(hit, axis=1, keepdims=True).astype(jnp.int32) - 1
    index = index[:, :1]
    place = jnp.where((place >= 0) & (index >= capacity), place + held, place)
    place = jnp.where(index < 2 * capacity, place, -1)
    wanted = lax.broadcasted_iota(jnp.int32, (owners * rows, 2 * held), 1)
    route[...] = jnp.where(place == wanted, 1.0, 0.0).T.astype(jnp.bfloat16)
    route_out = pltpu.make_async_copy(route, route_ref, local_sem.at[6])
    route_out.start()

    grad = grad_own[my_x].astype(jnp.float32) + grad_pair[my_x].astype(jnp.float32)
    for step in range(1, n_x):
        grad_copy(step).wait_send()
        grad_arrival(step).wait_recv()
        grad = grad + grad_in[lax.rem(my_x + step, n_x)].astype(jnp.float32)
    total[...] = grad
    total_out = pltpu.make_async_copy(total, total_ref, local_sem.at[7])
    total_out.start()

    def finish(step, carry):
        other = lax.rem(myself + step, owners)
        copy = copy_to(other // n_tensor, lax.rem(other, n_tensor), other, other, other)
        copy.wait_send()
        copy.wait_recv()
        return carry

    own_slots.wait()
    lax.fori_loop(1, owners, finish, 0)
    route_out.wait()
    total_out.wait()


def update(
    offset_ref,
    route_ref,
    arrived_ref,
    grad_ref,
    master_ref,
    m_codes_ref,
    m_scale_ref,
    v_codes_ref,
    v_scale_ref,
    adam_ref,
    weight_ref,
    m_all,
    v_all,
    peaks,
):
    step = pl.program_id(0)
    held, width = master_ref.shape
    offset = offset_ref[0]
    placed = jnp.dot(route_ref[...], arrived_ref[...], preferred_element_type=jnp.float32)
    grad = grad_ref[...]
    m_next = FIRST_DECAY * placed[:held] + (1.0 - FIRST_DECAY) * grad
    v_next = SECOND_DECAY * placed[held:] + (1.0 - SECOND_DECAY) * grad * grad
    master = master_ref[...]
    adam = (m_next * (1.0 / FIRST_CORRECTION)) / (
        jnp.sqrt(v_next * (1.0 / SECOND_CORRECTION)) + ADAM_EPSILON
    ) + WEIGHT_DECAY * master
    adam_ref[...] = adam
    weight_ref[...] = (master - LEARN_RATE * adam).astype(jnp.bfloat16)
    m_all[step] = m_next
    v_all[step] = v_next
    column = lax.broadcasted_iota(jnp.int32, (held, width), 1)
    head = column < offset - step * width

    @pl.when(step == 0)
    def _():
        peaks[...] = jnp.zeros_like(peaks)

    for at, values in ((0, m_next), (2, v_next)):
        size = jnp.abs(values)
        fore = jnp.where(head, size, 0.0)
        rear = jnp.where(head, 0.0, size)
        for part, half in ((0, fore), (1, rear)):
            best = peaks[at + part]
            for lane in range(0, width, 128):
                best = jnp.maximum(best, half[:, lane : lane + 128])
            peaks[at + part] = best

    @pl.when(step == pl.num_programs(0) - 1)
    def _():
        line = lax.broadcasted_iota(jnp.int32, (held, held), 0)
        for at, values, codes_ref, scale_ref in (
            (0, m_all, m_codes_ref, m_scale_ref),
            (2, v_all, v_codes_ref, v_scale_ref),
        ):
            fore = jnp.broadcast_to(jnp.max(peaks[at], axis=1, keepdims=True), (held, held))
            rear = jnp.broadcast_to(jnp.max(peaks[at + 1], axis=1, keepdims=True), (held, held))
            above = jnp.where(line == 0, 0.0, pltpu.roll(rear, 1, 0))
            below = jnp.where(line == held - 1, 0.0, pltpu.roll(fore, held - 1, 0))
            first = jnp.maximum(above, fore) + 1e-06
            second = jnp.maximum(rear, below) + 1e-06
            scale_ref[:, :held] = first.T[:1, :]
            scale_ref[:, held : held + 1] = second[held - 1 :, :1]
            first = (1.0 / first)[:, :1]
            second = (1.0 / second)[:, :1]
            for part in range(values.shape[0]):
                left = column < offset - part * width
                codes_ref[:, part * width : (part + 1) * width] = (
                    values[part] * jnp.where(left, first, second)
                ).astype(jnp.bfloat16)


def local(
    n_dp,
    n_tensor,
    old_m_codes,
    old_m_scale,
    old_v_codes,
    old_v_scale,
    block_target,
    new_offset,
    grad_part,
    master_weight,
):
    owners = n_dp * n_tensor
    held, size = old_m_codes.shape
    capacity = max(2, 2 * held // owners)
    rows = -(-2 * capacity // 16) * 16
    hbm = pl.BlockSpec(memory_space=pl.ANY)
    n_x = n_dp // 2
    arrived, grad, route = pl.pallas_call(
        functools.partial(exchange, n_dp, n_tensor, capacity),
        out_shape=(
            jax.ShapeDtypeStruct((owners, rows, size), jnp.bfloat16),
            jax.ShapeDtypeStruct((held, size), jnp.float32),
            jax.ShapeDtypeStruct((2 * held, owners * rows), jnp.bfloat16),
        ),
        in_specs=[hbm] * 6,
        out_specs=(hbm, hbm, hbm),
        scratch_shapes=[
            pltpu.VMEM((owners, held), jnp.int32),
            pltpu.VMEM((held, size), jnp.bfloat16),
            pltpu.VMEM((1, held), jnp.float32),
            pltpu.VMEM((held, size), jnp.bfloat16),
            pltpu.VMEM((1, held), jnp.float32),
            pltpu.VMEM((owners, rows, size), jnp.bfloat16),
            pltpu.VMEM((n_x, held, size), jnp.bfloat16),
            pltpu.VMEM((n_x, held, size), jnp.bfloat16),
            pltpu.VMEM((n_x, held, size), jnp.bfloat16),
            pltpu.VMEM((n_x, held, size), jnp.bfloat16),
            pltpu.VMEM((held, size), jnp.float32),
            pltpu.VMEM((2 * held, owners * rows), jnp.bfloat16),
            pltpu.SemaphoreType.DMA((owners,)),
            pltpu.SemaphoreType.DMA((owners,)),
            pltpu.SemaphoreType.DMA((n_x,)),
            pltpu.SemaphoreType.DMA((n_x,)),
            pltpu.SemaphoreType.DMA((n_x,)),
            pltpu.SemaphoreType.DMA((n_x,)),
            pltpu.SemaphoreType.DMA((n_x,)),
            pltpu.SemaphoreType.DMA((8,)),
        ],
        compiler_params=pltpu.CompilerParams(
            collective_id=0, has_side_effects=True, vmem_limit_bytes=60 * 1024 * 1024
        ),
    )(
        block_target.reshape(owners, held),
        old_m_codes,
        old_m_scale.reshape(1, held),
        old_v_codes,
        old_v_scale.reshape(1, held),
        grad_part[0, 0],
    )
    width = 512
    whole = lambda shape: pl.BlockSpec(shape, lambda i: (0, 0))
    part = pl.BlockSpec((held, width), lambda i: (0, i))
    m_codes, m_scale, v_codes, v_scale, adam, weight = pl.pallas_call(
        update,
        grid=(size // width,),
        out_shape=(
            jax.ShapeDtypeStruct((held, size), jnp.bfloat16),
            jax.ShapeDtypeStruct((1, held + 1), jnp.float32),
            jax.ShapeDtypeStruct((held, size), jnp.bfloat16),
            jax.ShapeDtypeStruct((1, held + 1), jnp.float32),
            jax.ShapeDtypeStruct((held, size), jnp.float32),
            jax.ShapeDtypeStruct((held, size), jnp.bfloat16),
        ),
        in_specs=[
            pl.BlockSpec(memory_space=pltpu.SMEM),
            whole((2 * held, owners * rows)),
            pl.BlockSpec((owners * rows, width), lambda i: (0, i)),
            part,
            part,
        ],
        out_specs=(
            whole((held, size)),
            whole((1, held + 1)),
            whole((held, size)),
            whole((1, held + 1)),
            part,
            part,
        ),
        scratch_shapes=[
            pltpu.VMEM((size // width, held, width), jnp.float32),
            pltpu.VMEM((size // width, held, width), jnp.float32),
            pltpu.VMEM((4, held, 128), jnp.float32),
        ],
        compiler_params=pltpu.CompilerParams(
            dimension_semantics=("arbitrary",), vmem_limit_bytes=60 * 1024 * 1024
        ),
    )(
        new_offset,
        route,
        arrived.reshape(owners * rows, size),
        grad,
        master_weight[0],
    )
    return (
        m_codes.reshape(1, held, size),
        m_scale,
        v_codes.reshape(1, held, size),
        v_scale,
        adam.reshape(1, held, size),
        weight.reshape(1, held, size),
    )


def solution(mesh):
    return jax.shard_map(
        functools.partial(local, mesh.shape["dp"], mesh.shape["tensor"]),
        mesh=mesh,
        in_specs=(
            P(("dp", "tensor"), None),
            P(("dp", "tensor")),
            P(("dp", "tensor"), None),
            P(("dp", "tensor")),
            P(),
            P(("dp", "tensor")),
            P("dp", "tensor", None, None),
            P("tensor", "dp", None),
        ),
        out_specs=(
            P("tensor", "dp", None),
            P(("dp", "tensor"), None),
            P("tensor", "dp", None),
            P(("dp", "tensor"), None),
            P("tensor", "dp", None),
            P("tensor", "dp", None),
        ),
        check_vma=False,
    )
```

```python
import functools

import jax
import jax.numpy as jnp
from jax import lax
from jax.experimental import pallas as pl
from jax.experimental.pallas import tpu as pltpu
from jax.sharding import PartitionSpec as P

FIRST_DECAY = 0.9
SECOND_DECAY = 0.95
FIRST_CORRECTION = 1.0 - 0.9**40
SECOND_CORRECTION = 1.0 - 0.95**40
ADAM_EPSILON = 1e-08
WEIGHT_DECAY = 0.1
LEARN_RATE = 6e-05
MESH = pl.DeviceIdType.MESH


def column_of(row, held):
    return jnp.broadcast_to(row, (held, held)).T


def exchange(
    n_dp,
    n_tensor,
    capacity,
    targets_hbm,
    m_codes_hbm,
    m_scale_hbm,
    v_codes_hbm,
    v_scale_hbm,
    grad_ref,
    arrived_ref,
    total_ref,
    route_ref,
    targets_ref,
    m_codes_ref,
    m_scale_ref,
    v_codes_ref,
    v_scale_ref,
    outgoing,
    grad_own,
    grad_pair,
    grad_out,
    grad_in,
    total,
    route,
    send_sem,
    recv_sem,
    pair_send_sem,
    pair_recv_sem,
    grad_send_sem,
    grad_recv_sem,
    own_sem,
    local_sem,
):
    owners = n_dp * n_tensor
    held, size = m_codes_ref.shape
    rows = outgoing.shape[1]
    n_x = n_dp // 2
    my_dp = lax.axis_index("dp")
    my_tensor = lax.axis_index("tensor")
    myself = my_dp * n_tensor + my_tensor
    my_x = my_dp // 2
    my_core = lax.rem(my_dp, 2)

    barrier = pltpu.get_barrier_semaphore()

    def greet(step, carry):
        other = lax.rem(myself + step, owners)
        pl.semaphore_signal(
            barrier, inc=1, device_id=(other // n_tensor, lax.rem(other, n_tensor)), device_id_type=MESH
        )
        return carry

    loads = [
        pltpu.make_async_copy(source, target, local_sem.at[i])
        for i, (source, target) in enumerate(
            (
                (targets_hbm, targets_ref),
                (m_scale_hbm, m_scale_ref),
                (v_scale_hbm, v_scale_ref),
                (m_codes_hbm, m_codes_ref),
                (v_codes_hbm, v_codes_ref),
            )
        )
    ]
    for load in loads:
        load.start()
    lax.fori_loop(1, owners, greet, 0)

    def share(x, core):
        return grad_ref.at[pl.ds(pl.multiple_of((2 * x + core) * held, held), held)]

    own_loads = [
        pltpu.make_async_copy(share(x, my_core), grad_own.at[x], own_sem.at[x]) for x in range(n_x)
    ]
    for load in own_loads:
        load.start()

    loads[0].wait()
    mine = targets_ref[pl.ds(myself, 1), :]
    owner = (mine // held).astype(jnp.float32)
    owner_col = column_of(owner, held)
    owner_row = jnp.broadcast_to(owner, (held, held))
    down = lax.broadcasted_iota(jnp.int32, (held, held), 0)
    across = lax.broadcasted_iota(jnp.int32, (held, held), 1)
    rank = jnp.sum(
        jnp.where((owner_col == owner_row) & (down < across), 1.0, 0.0), axis=0, keepdims=True
    )
    slot = (owner * rows + rank).astype(jnp.int32)
    slots = jnp.concatenate([slot, slot + capacity], axis=1)
    for load in loads[1:]:
        load.wait()
    m_old = m_codes_ref[...].astype(jnp.float32) * column_of(m_scale_ref[...], held)[:, :1]
    v_old = v_codes_ref[...].astype(jnp.float32) * column_of(v_scale_ref[...], held)[:, :1]
    moments = jnp.concatenate([m_old.astype(jnp.bfloat16), v_old.astype(jnp.bfloat16)], axis=0)

    pair_copies = [
        pltpu.make_async_remote_copy(
            src_ref=share(x, 1 - my_core),
            dst_ref=grad_pair.at[x],
            send_sem=pair_send_sem.at[x],
            recv_sem=pair_recv_sem.at[x],
            device_id=(2 * my_x + 1 - my_core, my_tensor),
            device_id_type=MESH,
        )
        for x in range(n_x)
    ]

    def grad_copy(step):
        other = lax.rem(my_x + step, n_x)
        return pltpu.make_async_remote_copy(
            src_ref=grad_out.at[other],
            dst_ref=grad_in.at[my_x],
            send_sem=grad_send_sem.at[other],
            recv_sem=grad_recv_sem.at[my_x],
            device_id=(2 * other + my_core, my_tensor),
            device_id_type=MESH,
        )

    def grad_arrival(step):
        other = lax.rem(my_x + step, n_x)
        return pltpu.make_async_remote_copy(
            src_ref=grad_out.at[other],
            dst_ref=grad_in.at[other],
            send_sem=grad_send_sem.at[other],
            recv_sem=grad_recv_sem.at[other],
            device_id=(2 * other + my_core, my_tensor),
            device_id_type=MESH,
        )

    def copy_to(there, lane, other, landing, arrival):
        return pltpu.make_async_remote_copy(
            src_ref=outgoing.at[other],
            dst_ref=arrived_ref.at[landing],
            send_sem=send_sem.at[other],
            recv_sem=recv_sem.at[arrival],
            device_id=(there, lane),
            device_id_type=MESH,
        )

    for group in range(n_dp):
        there = lax.rem(my_dp + group + 1, n_dp)
        base = there * n_tensor
        place = lax.broadcasted_iota(jnp.int32, (n_tensor * rows, 2 * held), 0) + base * rows
        chosen = jnp.where(place == slots, 1.0, 0.0).astype(jnp.bfloat16)
        packed = jnp.dot(chosen, moments, preferred_element_type=jnp.float32)
        outgoing[pl.ds(base, n_tensor)] = packed.astype(jnp.bfloat16).reshape(n_tensor, rows, size)
        if group == 0:
            pl.semaphore_wait(barrier, owners - 1)
            for copy in pair_copies:
                copy.start()
        last = group == n_dp - 1

        def send(step, carry, there=there, base=base):
            lane = lax.rem(my_tensor + step, n_tensor)
            copy_to(there, lane, base + lane, myself, myself).start()
            return carry

        half = n_tensor // 2
        if group < n_dp - 1:
            lax.fori_loop(0, half, send, 0)
        else:
            lax.fori_loop(1, half, send, 0)

            def far(step, carry):
                for back in range(n_dp):
                    there2 = lax.rem(my_dp + back + 1, n_dp)
                    send(step, 0, there=there2, base=there2 * n_tensor)
                return carry

            lax.fori_loop(half, n_tensor, far, 0)
    own_slots = pltpu.make_async_copy(outgoing.at[myself], arrived_ref.at[myself], local_sem.at[5])
    own_slots.start()

    for load in own_loads:
        load.wait()
    for copy in pair_copies:
        copy.wait_send()
        copy.wait_recv()
    for step in range(1, n_x):
        other = lax.rem(my_x + step, n_x)
        grad_out[other] = (
            grad_own[other].astype(jnp.float32) + grad_pair[other].astype(jnp.float32)
        ).astype(jnp.bfloat16)
        grad_copy(step).start()

    targets = targets_ref[...]
    is_mine = jnp.where(targets // held == myself, 1.0, 0.0)
    before = jnp.where(down < across, 1.0, 0.0).astype(jnp.bfloat16)
    ranks = jnp.dot(is_mine.astype(jnp.bfloat16), before, preferred_element_type=jnp.float32)
    ranks = jnp.where(is_mine > 0.0, ranks, -1.0)
    row = lax.rem(targets, held).astype(jnp.float32) + 1.0

    def spread(x):
        return jnp.broadcast_to(x[:, None, :], (owners, rows, held)).reshape(owners * rows, held)

    index = lax.broadcasted_iota(jnp.int32, (owners, rows, held), 1).reshape(owners * rows, held)
    within = jnp.where(index >= capacity, index - capacity, index)
    hit = jnp.where(spread(ranks) == within.astype(jnp.float32), spread(row), 0.0)
    place = jnp.sum(hit, axis=1, keepdims=True).astype(jnp.int32) - 1
    index = index[:, :1]
    place = jnp.where((place >= 0) & (index >= capacity), place + held, place)
    place = jnp.where(index < 2 * capacity, place, -1)
    wanted = lax.broadcasted_iota(jnp.int32, (owners * rows, 2 * held), 1)
    route[...] = jnp.where(place == wanted, 1.0, 0.0).T.astype(jnp.bfloat16)
    route_out = pltpu.make_async_copy(route, route_ref, local_sem.at[6])
    route_out.start()

    grad = grad_own[my_x].astype(jnp.float32) + grad_pair[my_x].astype(jnp.float32)
    for step in range(1, n_x):
        grad_copy(step).wait_send()
        grad_arrival(step).wait_recv()
        grad = grad + grad_in[lax.rem(my_x + step, n_x)].astype(jnp.float32)
    total[...] = grad
    total_out = pltpu.make_async_copy(total, total_ref, local_sem.at[7])
    total_out.start()

    def finish(step, carry):
        other = lax.rem(myself + step, owners)
        copy = copy_to(other // n_tensor, lax.rem(other, n_tensor), other, other, other)
        copy.wait_send()
        copy.wait_recv()
        return carry

    own_slots.wait()
    lax.fori_loop(1, owners, finish, 0)
    route_out.wait()
    total_out.wait()


def update(
    offset_ref,
    route_ref,
    arrived_ref,
    grad_ref,
    master_ref,
    m_codes_ref,
    m_scale_ref,
    v_codes_ref,
    v_scale_ref,
    adam_ref,
    weight_ref,
    m_all,
    v_all,
    peaks,
):
    step = pl.program_id(0)
    held, width = master_ref.shape
    offset = offset_ref[0]
    placed = jnp.dot(route_ref[...], arrived_ref[...], preferred_element_type=jnp.float32)
    grad = grad_ref[...]
    m_next = FIRST_DECAY * placed[:held] + (1.0 - FIRST_DECAY) * grad
    v_next = SECOND_DECAY * placed[held:] + (1.0 - SECOND_DECAY) * grad * grad
    master = master_ref[...]
    adam = (m_next * (1.0 / FIRST_CORRECTION)) / (
        jnp.sqrt(v_next * (1.0 / SECOND_CORRECTION)) + ADAM_EPSILON
    ) + WEIGHT_DECAY * master
    adam_ref[...] = adam
    weight_ref[...] = (master - LEARN_RATE * adam).astype(jnp.bfloat16)
    m_all[step] = m_next
    v_all[step] = v_next
    column = lax.broadcasted_iota(jnp.int32, (held, width), 1)
    head = column < offset - step * width

    @pl.when(step == 0)
    def _():
        peaks[...] = jnp.zeros_like(peaks)

    for at, values in ((0, m_next), (2, v_next)):
        size = jnp.abs(values)
        fore = jnp.where(head, size, 0.0)
        rear = jnp.where(head, 0.0, size)
        for part, half in ((0, fore), (1, rear)):
            best = peaks[at + part]
            for lane in range(0, width, 128):
                best = jnp.maximum(best, half[:, lane : lane + 128])
            peaks[at + part] = best

    @pl.when(step == pl.num_programs(0) - 1)
    def _():
        line = lax.broadcasted_iota(jnp.int32, (held, held), 0)
        for at, values, codes_ref, scale_ref in (
            (0, m_all, m_codes_ref, m_scale_ref),
            (2, v_all, v_codes_ref, v_scale_ref),
        ):
            fore = jnp.broadcast_to(jnp.max(peaks[at], axis=1, keepdims=True), (held, held))
            rear = jnp.broadcast_to(jnp.max(peaks[at + 1], axis=1, keepdims=True), (held, held))
            above = jnp.where(line == 0, 0.0, pltpu.roll(rear, 1, 0))
            below = jnp.where(line == held - 1, 0.0, pltpu.roll(fore, held - 1, 0))
            first = jnp.maximum(above, fore) + 1e-06
            second = jnp.maximum(rear, below) + 1e-06
            scale_ref[:, :held] = first.T[:1, :]
            scale_ref[:, held : held + 1] = second[held - 1 :, :1]
            first = (1.0 / first)[:, :1]
            second = (1.0 / second)[:, :1]
            for part in range(values.shape[0]):
                left = column < offset - part * width
                codes_ref[:, part * width : (part + 1) * width] = (
                    values[part] * jnp.where(left, first, second)
                ).astype(jnp.bfloat16)


def local(
    n_dp,
    n_tensor,
    old_m_codes,
    old_m_scale,
    old_v_codes,
    old_v_scale,
    block_target,
    new_offset,
    grad_part,
    master_weight,
):
    owners = n_dp * n_tensor
    held, size = old_m_codes.shape
    capacity = max(2, 2 * held // owners)
    rows = -(-2 * capacity // 16) * 16
    hbm = pl.BlockSpec(memory_space=pl.ANY)
    n_x = n_dp // 2
    arrived, grad, route = pl.pallas_call(
        functools.partial(exchange, n_dp, n_tensor, capacity),
        out_shape=(
            jax.ShapeDtypeStruct((owners, rows, size), jnp.bfloat16),
            jax.ShapeDtypeStruct((held, size), jnp.float32),
            jax.ShapeDtypeStruct((2 * held, owners * rows), jnp.bfloat16),
        ),
        in_specs=[hbm] * 6,
        out_specs=(hbm, hbm, hbm),
        scratch_shapes=[
            pltpu.VMEM((owners, held), jnp.int32),
            pltpu.VMEM((held, size), jnp.bfloat16),
            pltpu.VMEM((1, held), jnp.float32),
            pltpu.VMEM((held, size), jnp.bfloat16),
            pltpu.VMEM((1, held), jnp.float32),
            pltpu.VMEM((owners, rows, size), jnp.bfloat16),
            pltpu.VMEM((n_x, held, size), jnp.bfloat16),
            pltpu.VMEM((n_x, held, size), jnp.bfloat16),
            pltpu.VMEM((n_x, held, size), jnp.bfloat16),
            pltpu.VMEM((n_x, held, size), jnp.bfloat16),
            pltpu.VMEM((held, size), jnp.float32),
            pltpu.VMEM((2 * held, owners * rows), jnp.bfloat16),
            pltpu.SemaphoreType.DMA((owners,)),
            pltpu.SemaphoreType.DMA((owners,)),
            pltpu.SemaphoreType.DMA((n_x,)),
            pltpu.SemaphoreType.DMA((n_x,)),
            pltpu.SemaphoreType.DMA((n_x,)),
            pltpu.SemaphoreType.DMA((n_x,)),
            pltpu.SemaphoreType.DMA((n_x,)),
            pltpu.SemaphoreType.DMA((8,)),
        ],
        compiler_params=pltpu.CompilerParams(
            collective_id=0, has_side_effects=True, vmem_limit_bytes=60 * 1024 * 1024
        ),
    )(
        block_target.reshape(owners, held),
        old_m_codes,
        old_m_scale.reshape(1, held),
        old_v_codes,
        old_v_scale.reshape(1, held),
        grad_part[0, 0],
    )
    width = 1024
    whole = lambda shape: pl.BlockSpec(shape, lambda i: (0, 0))
    part = pl.BlockSpec((held, width), lambda i: (0, i))
    m_codes, m_scale, v_codes, v_scale, adam, weight = pl.pallas_call(
        update,
        grid=(size // width,),
        out_shape=(
            jax.ShapeDtypeStruct((held, size), jnp.bfloat16),
            jax.ShapeDtypeStruct((1, held + 1), jnp.float32),
            jax.ShapeDtypeStruct((held, size), jnp.bfloat16),
            jax.ShapeDtypeStruct((1, held + 1), jnp.float32),
            jax.ShapeDtypeStruct((held, size), jnp.float32),
            jax.ShapeDtypeStruct((held, size), jnp.bfloat16),
        ),
        in_specs=[
            pl.BlockSpec(memory_space=pltpu.SMEM),
            whole((2 * held, owners * rows)),
            pl.BlockSpec((owners * rows, width), lambda i: (0, i)),
            part,
            part,
        ],
        out_specs=(
            whole((held, size)),
            whole((1, held + 1)),
            whole((held, size)),
            whole((1, held + 1)),
            part,
            part,
        ),
        scratch_shapes=[
            pltpu.VMEM((size // width, held, width), jnp.float32),
            pltpu.VMEM((size // width, held, width), jnp.float32),
            pltpu.VMEM((4, held, 128), jnp.float32),
        ],
        compiler_params=pltpu.CompilerParams(
            dimension_semantics=("arbitrary",), vmem_limit_bytes=60 * 1024 * 1024
        ),
    )(
        new_offset,
        route,
        arrived.reshape(owners * rows, size),
        grad,
        master_weight[0],
    )
    return (
        m_codes.reshape(1, held, size),
        m_scale,
        v_codes.reshape(1, held, size),
        v_scale,
        adam.reshape(1, held, size),
        weight.reshape(1, held, size),
    )


def solution(mesh):
    return jax.shard_map(
        functools.partial(local, mesh.shape["dp"], mesh.shape["tensor"]),
        mesh=mesh,
        in_specs=(
            P(("dp", "tensor"), None),
            P(("dp", "tensor")),
            P(("dp", "tensor"), None),
            P(("dp", "tensor")),
            P(),
            P(("dp", "tensor")),
            P("dp", "tensor", None, None),
            P("tensor", "dp", None),
        ),
        out_specs=(
            P("tensor", "dp", None),
            P(("dp", "tensor"), None),
            P("tensor", "dp", None),
            P(("dp", "tensor"), None),
            P("tensor", "dp", None),
            P("tensor", "dp", None),
        ),
        check_vma=False,
    )
```

```python
import functools

import jax
import jax.numpy as jnp
from jax import lax
from jax.experimental import pallas as pl
from jax.experimental.pallas import tpu as pltpu
from jax.sharding import PartitionSpec as P

FIRST_DECAY = 0.9
SECOND_DECAY = 0.95
FIRST_CORRECTION = 1.0 - 0.9**40
SECOND_CORRECTION = 1.0 - 0.95**40
ADAM_EPSILON = 1e-08
WEIGHT_DECAY = 0.1
LEARN_RATE = 6e-05
MESH = pl.DeviceIdType.MESH


def column_of(row, held):
    return jnp.broadcast_to(row, (held, held)).T


def exchange(
    n_dp,
    n_tensor,
    capacity,
    targets_hbm,
    m_codes_hbm,
    m_scale_hbm,
    v_codes_hbm,
    v_scale_hbm,
    grad_ref,
    arrived_ref,
    total_ref,
    route_ref,
    targets_ref,
    m_codes_ref,
    m_scale_ref,
    v_codes_ref,
    v_scale_ref,
    outgoing,
    grad_own,
    grad_pair,
    grad_out,
    grad_in,
    total,
    route,
    send_sem,
    recv_sem,
    pair_send_sem,
    pair_recv_sem,
    grad_send_sem,
    grad_recv_sem,
    own_sem,
    local_sem,
):
    owners = n_dp * n_tensor
    held, size = m_codes_ref.shape
    rows = outgoing.shape[1]
    n_x = n_dp // 2
    my_dp = lax.axis_index("dp")
    my_tensor = lax.axis_index("tensor")
    myself = my_dp * n_tensor + my_tensor
    my_x = my_dp // 2
    my_core = lax.rem(my_dp, 2)

    barrier = pltpu.get_barrier_semaphore()

    def greet(step, carry):
        other = lax.rem(myself + step, owners)
        pl.semaphore_signal(
            barrier, inc=1, device_id=(other // n_tensor, lax.rem(other, n_tensor)), device_id_type=MESH
        )
        return carry

    loads = [
        pltpu.make_async_copy(source, target, local_sem.at[i])
        for i, (source, target) in enumerate(
            (
                (targets_hbm, targets_ref),
                (m_scale_hbm, m_scale_ref),
                (v_scale_hbm, v_scale_ref),
                (m_codes_hbm, m_codes_ref),
                (v_codes_hbm, v_codes_ref),
            )
        )
    ]
    for load in loads:
        load.start()
    lax.fori_loop(1, owners, greet, 0)

    def share(x, core):
        return grad_ref.at[pl.ds(pl.multiple_of((2 * x + core) * held, held), held)]

    own_loads = [
        pltpu.make_async_copy(share(x, my_core), grad_own.at[x], own_sem.at[x]) for x in range(n_x)
    ]
    for load in own_loads:
        load.start()

    loads[0].wait()
    mine = targets_ref[pl.ds(myself, 1), :]
    owner = (mine // held).astype(jnp.float32)
    owner_col = column_of(owner, held)
    owner_row = jnp.broadcast_to(owner, (held, held))
    down = lax.broadcasted_iota(jnp.int32, (held, held), 0)
    across = lax.broadcasted_iota(jnp.int32, (held, held), 1)
    rank = jnp.sum(
        jnp.where((owner_col == owner_row) & (down < across), 1.0, 0.0), axis=0, keepdims=True
    )
    slot = (owner * rows + rank).astype(jnp.int32)
    slots = jnp.concatenate([slot, slot + capacity], axis=1)
    for load in loads[1:]:
        load.wait()
    m_old = m_codes_ref[...].astype(jnp.float32) * column_of(m_scale_ref[...], held)[:, :1]
    v_old = v_codes_ref[...].astype(jnp.float32) * column_of(v_scale_ref[...], held)[:, :1]
    moments = jnp.concatenate([m_old.astype(jnp.bfloat16), v_old.astype(jnp.bfloat16)], axis=0)

    pair_copies = [
        pltpu.make_async_remote_copy(
            src_ref=share(x, 1 - my_core),
            dst_ref=grad_pair.at[x],
            send_sem=pair_send_sem.at[x],
            recv_sem=pair_recv_sem.at[x],
            device_id=(2 * my_x + 1 - my_core, my_tensor),
            device_id_type=MESH,
        )
        for x in range(n_x)
    ]

    def grad_copy(step):
        other = lax.rem(my_x + step, n_x)
        return pltpu.make_async_remote_copy(
            src_ref=grad_out.at[other],
            dst_ref=grad_in.at[my_x],
            send_sem=grad_send_sem.at[other],
            recv_sem=grad_recv_sem.at[my_x],
            device_id=(2 * other + my_core, my_tensor),
            device_id_type=MESH,
        )

    def grad_arrival(step):
        other = lax.rem(my_x + step, n_x)
        return pltpu.make_async_remote_copy(
            src_ref=grad_out.at[other],
            dst_ref=grad_in.at[other],
            send_sem=grad_send_sem.at[other],
            recv_sem=grad_recv_sem.at[other],
            device_id=(2 * other + my_core, my_tensor),
            device_id_type=MESH,
        )

    def copy_to(there, lane, other, landing, arrival):
        return pltpu.make_async_remote_copy(
            src_ref=outgoing.at[other],
            dst_ref=arrived_ref.at[landing],
            send_sem=send_sem.at[other],
            recv_sem=recv_sem.at[arrival],
            device_id=(there, lane),
            device_id_type=MESH,
        )

    for group in range(n_dp):
        there = lax.rem(my_dp + group + 1, n_dp)
        base = there * n_tensor
        place = lax.broadcasted_iota(jnp.int32, (n_tensor * rows, 2 * held), 0) + base * rows
        chosen = jnp.where(place == slots, 1.0, 0.0).astype(jnp.bfloat16)
        packed = jnp.dot(chosen, moments, preferred_element_type=jnp.float32)
        outgoing[pl.ds(base, n_tensor)] = packed.astype(jnp.bfloat16).reshape(n_tensor, rows, size)
        if group == 0:
            pl.semaphore_wait(barrier, owners - 1)
            for copy in pair_copies:
                copy.start()
        last = group == n_dp - 1

        def send(step, carry, there=there, base=base):
            lane = lax.rem(my_tensor + step, n_tensor)
            copy_to(there, lane, base + lane, myself, myself).start()
            return carry

        half = n_tensor // 2
        if group < n_dp - 1:
            lax.fori_loop(0, half, send, 0)
        else:
            lax.fori_loop(1, half, send, 0)

            def far(step, carry):
                for back in range(n_dp):
                    there2 = lax.rem(my_dp + back + 1, n_dp)
                    send(step, 0, there=there2, base=there2 * n_tensor)
                return carry

            lax.fori_loop(half, n_tensor, far, 0)
    own_slots = pltpu.make_async_copy(outgoing.at[myself], arrived_ref.at[myself], local_sem.at[5])
    own_slots.start()

    for load in own_loads:
        load.wait()
    for copy in pair_copies:
        copy.wait_send()
        copy.wait_recv()
    for step in range(1, n_x):
        other = lax.rem(my_x + step, n_x)
        grad_out[other] = (
            grad_own[other].astype(jnp.float32) + grad_pair[other].astype(jnp.float32)
        ).astype(jnp.bfloat16)
        grad_copy(step).start()

    targets = targets_ref[...]
    is_mine = jnp.where(targets // held == myself, 1.0, 0.0)
    before = jnp.where(down < across, 1.0, 0.0).astype(jnp.bfloat16)
    ranks = jnp.dot(is_mine.astype(jnp.bfloat16), before, preferred_element_type=jnp.float32)
    ranks = jnp.where(is_mine > 0.0, ranks, -1.0)
    row = lax.rem(targets, held).astype(jnp.float32) + 1.0

    def spread(x):
        return jnp.broadcast_to(x[:, None, :], (owners, rows, held)).reshape(owners * rows, held)

    index = lax.broadcasted_iota(jnp.int32, (owners, rows, held), 1).reshape(owners * rows, held)
    within = jnp.where(index >= capacity, index - capacity, index)
    hit = jnp.where(spread(ranks) == within.astype(jnp.float32), spread(row), 0.0)
    place = jnp.sum(hit, axis=1, keepdims=True).astype(jnp.int32) - 1
    index = index[:, :1]
    place = jnp.where((place >= 0) & (index >= capacity), place + held, place)
    place = jnp.where(index < 2 * capacity, place, -1)
    wanted = lax.broadcasted_iota(jnp.int32, (owners * rows, 2 * held), 1)
    route[...] = jnp.where(place == wanted, 1.0, 0.0).T.astype(jnp.bfloat16)
    route_out = pltpu.make_async_copy(route, route_ref, local_sem.at[6])
    route_out.start()

    grad = grad_own[my_x].astype(jnp.float32) + grad_pair[my_x].astype(jnp.float32)
    for step in range(1, n_x):
        grad_copy(step).wait_send()
        grad_arrival(step).wait_recv()
        grad = grad + grad_in[lax.rem(my_x + step, n_x)].astype(jnp.float32)
    total[...] = grad
    total_out = pltpu.make_async_copy(total, total_ref, local_sem.at[7])
    total_out.start()

    def finish(step, carry):
        other = lax.rem(myself + step, owners)
        copy = copy_to(other // n_tensor, lax.rem(other, n_tensor), other, other, other)
        copy.wait_send()
        copy.wait_recv()
        return carry

    own_slots.wait()
    lax.fori_loop(1, owners, finish, 0)
    route_out.wait()
    total_out.wait()


def update(
    offset_ref,
    route_ref,
    arrived_ref,
    grad_ref,
    master_ref,
    m_codes_ref,
    m_scale_ref,
    v_codes_ref,
    v_scale_ref,
    adam_ref,
    weight_ref,
    m_all,
    v_all,
    peaks,
):
    step = pl.program_id(0)
    held, width = master_ref.shape
    offset = offset_ref[0]
    placed = jnp.dot(route_ref[...], arrived_ref[...], preferred_element_type=jnp.float32)
    grad = grad_ref[...]
    m_next = FIRST_DECAY * placed[:held] + (1.0 - FIRST_DECAY) * grad
    v_next = SECOND_DECAY * placed[held:] + (1.0 - SECOND_DECAY) * grad * grad
    master = master_ref[...]
    adam = (m_next * (1.0 / FIRST_CORRECTION)) / (
        jnp.sqrt(v_next * (1.0 / SECOND_CORRECTION)) + ADAM_EPSILON
    ) + WEIGHT_DECAY * master
    adam_ref[...] = adam
    weight_ref[...] = (master - LEARN_RATE * adam).astype(jnp.bfloat16)
    m_all[step] = m_next
    v_all[step] = v_next
    column = lax.broadcasted_iota(jnp.int32, (held, width), 1)
    head = column < offset - step * width

    @pl.when(step == 0)
    def _():
        peaks[...] = jnp.zeros_like(peaks)

    for at, values in ((0, m_next), (2, v_next)):
        size = jnp.abs(values)
        fore = jnp.where(head, size, 0.0)
        rear = jnp.where(head, 0.0, size)
        for part, half in ((0, fore), (1, rear)):
            best = peaks[at + part]
            for lane in range(0, width, 128):
                best = jnp.maximum(best, half[:, lane : lane + 128])
            peaks[at + part] = best

    @pl.when(step == pl.num_programs(0) - 1)
    def _():
        line = lax.broadcasted_iota(jnp.int32, (held, held), 0)
        for at, values, codes_ref, scale_ref in (
            (0, m_all, m_codes_ref, m_scale_ref),
            (2, v_all, v_codes_ref, v_scale_ref),
        ):
            fore = jnp.broadcast_to(jnp.max(peaks[at], axis=1, keepdims=True), (held, held))
            rear = jnp.broadcast_to(jnp.max(peaks[at + 1], axis=1, keepdims=True), (held, held))
            above = jnp.where(line == 0, 0.0, pltpu.roll(rear, 1, 0))
            below = jnp.where(line == held - 1, 0.0, pltpu.roll(fore, held - 1, 0))
            first = jnp.maximum(above, fore) + 1e-06
            second = jnp.maximum(rear, below) + 1e-06
            scale_ref[:, :held] = first.T[:1, :]
            scale_ref[:, held : held + 1] = second[held - 1 :, :1]
            first = (1.0 / first)[:, :1]
            second = (1.0 / second)[:, :1]
            for part in range(values.shape[0]):
                left = column < offset - part * width
                codes_ref[:, part * width : (part + 1) * width] = (
                    values[part] * jnp.where(left, first, second)
                ).astype(jnp.bfloat16)


def local(
    n_dp,
    n_tensor,
    old_m_codes,
    old_m_scale,
    old_v_codes,
    old_v_scale,
    block_target,
    new_offset,
    grad_part,
    master_weight,
):
    owners = n_dp * n_tensor
    held, size = old_m_codes.shape
    capacity = max(2, 2 * held // owners)
    rows = -(-2 * capacity // 16) * 16
    hbm = pl.BlockSpec(memory_space=pl.ANY)
    n_x = n_dp // 2
    arrived, grad, route = pl.pallas_call(
        functools.partial(exchange, n_dp, n_tensor, capacity),
        out_shape=(
            jax.ShapeDtypeStruct((owners, rows, size), jnp.bfloat16),
            jax.ShapeDtypeStruct((held, size), jnp.float32),
            jax.ShapeDtypeStruct((2 * held, owners * rows), jnp.bfloat16),
        ),
        in_specs=[hbm] * 6,
        out_specs=(hbm, hbm, hbm),
        scratch_shapes=[
            pltpu.VMEM((owners, held), jnp.int32),
            pltpu.VMEM((held, size), jnp.bfloat16),
            pltpu.VMEM((1, held), jnp.float32),
            pltpu.VMEM((held, size), jnp.bfloat16),
            pltpu.VMEM((1, held), jnp.float32),
            pltpu.VMEM((owners, rows, size), jnp.bfloat16),
            pltpu.VMEM((n_x, held, size), jnp.bfloat16),
            pltpu.VMEM((n_x, held, size), jnp.bfloat16),
            pltpu.VMEM((n_x, held, size), jnp.bfloat16),
            pltpu.VMEM((n_x, held, size), jnp.bfloat16),
            pltpu.VMEM((held, size), jnp.float32),
            pltpu.VMEM((2 * held, owners * rows), jnp.bfloat16),
            pltpu.SemaphoreType.DMA((owners,)),
            pltpu.SemaphoreType.DMA((owners,)),
            pltpu.SemaphoreType.DMA((n_x,)),
            pltpu.SemaphoreType.DMA((n_x,)),
            pltpu.SemaphoreType.DMA((n_x,)),
            pltpu.SemaphoreType.DMA((n_x,)),
            pltpu.SemaphoreType.DMA((n_x,)),
            pltpu.SemaphoreType.DMA((8,)),
        ],
        compiler_params=pltpu.CompilerParams(
            collective_id=0, has_side_effects=True, vmem_limit_bytes=60 * 1024 * 1024
        ),
    )(
        block_target.reshape(owners, held),
        old_m_codes,
        old_m_scale.reshape(1, held),
        old_v_codes,
        old_v_scale.reshape(1, held),
        grad_part[0, 0],
    )
    width = 2048
    whole = lambda shape: pl.BlockSpec(shape, lambda i: (0, 0))
    part = pl.BlockSpec((held, width), lambda i: (0, i))
    m_codes, m_scale, v_codes, v_scale, adam, weight = pl.pallas_call(
        update,
        grid=(size // width,),
        out_shape=(
            jax.ShapeDtypeStruct((held, size), jnp.bfloat16),
            jax.ShapeDtypeStruct((1, held + 1), jnp.float32),
            jax.ShapeDtypeStruct((held, size), jnp.bfloat16),
            jax.ShapeDtypeStruct((1, held + 1), jnp.float32),
            jax.ShapeDtypeStruct((held, size), jnp.float32),
            jax.ShapeDtypeStruct((held, size), jnp.bfloat16),
        ),
        in_specs=[
            pl.BlockSpec(memory_space=pltpu.SMEM),
            whole((2 * held, owners * rows)),
            pl.BlockSpec((owners * rows, width), lambda i: (0, i)),
            part,
            part,
        ],
        out_specs=(
            whole((held, size)),
            whole((1, held + 1)),
            whole((held, size)),
            whole((1, held + 1)),
            part,
            part,
        ),
        scratch_shapes=[
            pltpu.VMEM((size // width, held, width), jnp.float32),
            pltpu.VMEM((size // width, held, width), jnp.float32),
            pltpu.VMEM((4, held, 128), jnp.float32),
        ],
        compiler_params=pltpu.CompilerParams(
            dimension_semantics=("arbitrary",), vmem_limit_bytes=60 * 1024 * 1024
        ),
    )(
        new_offset,
        route,
        arrived.reshape(owners * rows, size),
        grad,
        master_weight[0],
    )
    return (
        m_codes.reshape(1, held, size),
        m_scale,
        v_codes.reshape(1, held, size),
        v_scale,
        adam.reshape(1, held, size),
        weight.reshape(1, held, size),
    )


def solution(mesh):
    return jax.shard_map(
        functools.partial(local, mesh.shape["dp"], mesh.shape["tensor"]),
        mesh=mesh,
        in_specs=(
            P(("dp", "tensor"), None),
            P(("dp", "tensor")),
            P(("dp", "tensor"), None),
            P(("dp", "tensor")),
            P(),
            P(("dp", "tensor")),
            P("dp", "tensor", None, None),
            P("tensor", "dp", None),
        ),
        out_specs=(
            P("tensor", "dp", None),
            P(("dp", "tensor"), None),
            P("tensor", "dp", None),
            P(("dp", "tensor"), None),
            P("tensor", "dp", None),
            P("tensor", "dp", None),
        ),
        check_vma=False,
    )
```
